32 devices in a mesh: dx: 16 (over z, x, core), dy: 2 (over y).
Axes of the slice: x: 2, y: 2, z: 4, core: 2. Of those that a mesh axis runs over, the one named last changes fastest.
Arguments:
- img_emb: bfloat16 [16384, 1152], P(('dx', 'dy')), may hold values from -0.1796875 to 0.1796875
- txt_emb: bfloat16 [16384, 1152], P(('dx', 'dy')), may hold values from -0.1796875 to 0.1796875
- logit_scale: float32 [1], replicated, may hold values from 4 to 8
- logit_bias: float32 [1], replicated, may hold values from -3 to -1
Outputs:
- grad_img: float32 [16384, 1152], P(('dx', 'dy'))
- grad_txt: float32 [16384, 1152], P(('dx', 'dy'))
The draws below stay inside these ranges and needn't reach their ends.
All inputs are finite; a program needn't handle non-finite values.
Results may differ from the reference program's by a relative error of at most 0.0049.
Values may be sent and summed in bfloat16 or wider, within the bound.
No kernel may reach another device: no remote copies, remote signals or barrier semaphores. Data moves between devices by JAX's collectives and lax.ppermute only.
A program may use at most 64 MiB of HBM per device.

```python
import jax
import jax.numpy as jnp
from jax import lax

E = 1152
ROWS = 512
PAIRS = 16384
N_DX = 16
N_DY = 2


def levels(own_key, dims, pieces, least, top_value):
    factor_of, own = 1.0, jax.random.fold_in(own_key, 6)
    for axis_at, blocks in pieces:
        draws = jnp.exp(jax.random.uniform(jax.random.fold_in(own, axis_at), (blocks,), jnp.float32, least / len(pieces), top_value / len(pieces)))
        factor_of = factor_of * jnp.repeat(draws, dims[axis_at] // blocks).reshape([-1 if axis == axis_at else 1 for axis in range(len(dims))])
    return factor_of


def normal_values(rng, dims, scale, limit, split=(), held_as=jnp.bfloat16):
    array = jax.random.normal(rng, dims, jnp.float32) * scale
    if len(split) > 0:
        array = levels(rng, dims, split, -0.22, 0.18) * array
    return jnp.clip(array, min=-limit, max=limit).astype(held_as)


def setup_inputs(seed: int = 0) -> dict:
    keys = jax.random.split(jax.random.key(seed), 5)
    return {
        "img_emb": normal_values(keys[0], (PAIRS, E), 0.03, 0.1796875, ((0, 32),)),
        "txt_emb": normal_values(keys[1], (PAIRS, E), 0.03, 0.1796875, ((0, 32),)),
        "logit_scale": jnp.clip(jax.random.uniform(keys[2], (1,), jnp.float32, 4.0, 8.0), 4.0, 8.0),
        "logit_bias": jnp.clip(jax.random.uniform(keys[3], (1,), jnp.float32, -3.0, -1.0), -3.0, -1.0),
    }


def normalize(values):
    floats = values.astype(jnp.float32)
    inverse = lax.rsqrt(lax.optimization_barrier(jnp.sum(floats * floats, axis=-1, keepdims=True)) + 1e-06)
    return (floats * inverse, inverse)

def tile_weights(images, texts, scale, bias, diagonal):
    logits = scale * jnp.dot(images, texts.T, preferred_element_type=jnp.float32) + bias
    if diagonal:
        eye = jnp.arange(images.shape[0])[:, None] == jnp.arange(texts.shape[0])[None, :]
        signs = jnp.where(eye, jnp.float32(1.0), jnp.float32(-1.0))
    else:
        signs = jnp.full(logits.shape, -1.0, jnp.float32)
    coeffs = -signs * jax.nn.sigmoid(-signs * logits)
    return (scale * coeffs).astype(jnp.bfloat16)

def finish(unit, inverse, grads):
    return inverse * (grads - unit * lax.optimization_barrier(jnp.sum(unit * grads, axis=-1, keepdims=True)))

def reference(img_emb, txt_emb, logit_scale, logit_bias):
    blocks_all = N_DX * N_DY
    img_unit, inv_img = normalize(img_emb)
    txt_unit, inv_txt = normalize(txt_emb)
    img_b = img_unit.astype(jnp.bfloat16).reshape(blocks_all, ROWS, E)
    txt_b = txt_unit.astype(jnp.bfloat16).reshape(blocks_all, ROWS, E)
    scale = logit_scale[0]
    bias = logit_bias[0]

    def own_tile(blocks):
        images, texts = blocks
        coeffs = tile_weights(images, texts, scale, bias, True)
        return (jnp.dot(coeffs, texts, preferred_element_type=jnp.float32), jnp.dot(coeffs.T, images, preferred_element_type=jnp.float32))
    grad_i, grad_t = lax.map(own_tile, (img_b, txt_b))

    def cross_tile(blocks):
        images, texts = blocks
        coeffs = tile_weights(images, texts, scale, bias, False)
        return (jnp.dot(coeffs, texts, preferred_element_type=jnp.float32), jnp.dot(coeffs.T, images, preferred_element_type=jnp.float32).astype(jnp.bfloat16))
    for mask_value in [1, N_DY, N_DX // 2 * N_DY, 2 * N_DY]:
        partner = jnp.bitwise_xor(jnp.arange(blocks_all, dtype=jnp.int32), jnp.int32(mask_value))
        grad_more, partial_value = lax.map(cross_tile, (img_b, txt_b[partner]))
        partial_value = lax.optimization_barrier(partial_value)
        grad_i = grad_i + grad_more
        grad_t = grad_t + partial_value[partner].astype(jnp.float32)
    grad_i = grad_i.reshape(blocks_all * ROWS, E)
    grad_t = grad_t.reshape(blocks_all * ROWS, E)
    return (finish(img_unit, inv_img, grad_i), finish(txt_unit, inv_txt, grad_t))
```

```python
import functools

import jax
import jax.numpy as jnp
from jax import lax
from jax.experimental import pallas as pl
from jax.experimental.pallas import tpu as pltpu
from jax.sharding import PartitionSpec as P

STEP = 32


def unit_kernel(*refs):
    for values, rounded in zip(refs[:2], refs[2:]):
        floats = values[...].astype(jnp.float32)
        inverse = lax.rsqrt(jnp.sum(floats * floats, axis=-1, keepdims=True) + 1e-06)
        rounded[...] = (floats * inverse).astype(jnp.bfloat16)


def rounded_units(*arrays):
    rows, width = arrays[0].shape
    block = pl.BlockSpec((rows // 4, width), lambda i: (i, 0))
    shape = jax.ShapeDtypeStruct((rows, width), jnp.bfloat16)
    return pl.pallas_call(
        unit_kernel,
        grid=(4,),
        out_shape=(shape, shape),
        in_specs=[block, block],
        out_specs=(block, block),
    )(*arrays)


def add_kernel(offsets, odd, base, *refs):
    parts, (out, total, sems) = refs[: len(offsets) + (odd is not None)], refs[-3:]
    copies = []
    for index, offset in enumerate(offsets):
        for at in range(parts[index].shape[0] // STEP):
            here = pl.ds(at * STEP, STEP)
            there = pl.ds(offset + at * STEP, STEP)
            slot = pl.ds(len(copies) * STEP, STEP)
            part = parts[index][here].astype(jnp.float32)
            if odd is not None and index == len(offsets) - 1:
                is_odd = odd(lax.axis_index("dx")) == 1
                part = jnp.where(is_odd, parts[index + 1][here].astype(jnp.float32), part)
            total[slot] = base[there] + part
            copies.append(
                pltpu.make_async_copy(total.at[slot], out.at[there], sems.at[len(copies)])
            )
            copies[-1].start()
    for copy in copies:
        copy.wait()


def add_rows(base, parts, offsets, out=None, odd=None):
    vmem, hbm = (pl.BlockSpec(memory_space=space) for space in (pltpu.VMEM, pltpu.HBM))
    args = [base, *parts] + ([] if out is None else [out])
    rows = sum(part.shape[0] for part in parts[: len(offsets)])
    return pl.pallas_call(
        functools.partial(add_kernel, offsets, odd),
        out_shape=jax.ShapeDtypeStruct(base.shape, jnp.float32),
        in_specs=[vmem] * (1 + len(parts)) + ([] if out is None else [hbm]),
        out_specs=hbm,
        scratch_shapes=[
            pltpu.VMEM((rows, base.shape[1]), jnp.float32),
            pltpu.SemaphoreType.DMA((rows // STEP,)),
        ],
        input_output_aliases={} if out is None else {len(args) - 1: 0},
        compiler_params=pltpu.CompilerParams(vmem_limit_bytes=16 * 2**20),
        cost_estimate=pl.CostEstimate(
            flops=rows * base.shape[1], bytes_accessed=10 * rows * base.shape[1], transcendentals=0
        ),
    )(*args)


def from_partner(value, axis, stride, among=lambda index: True):
    pairs = [(i, i ^ 1 << stride) for i in range(lax.axis_size(axis)) if among(i)]
    return lax.ppermute(value, axis, pairs)


def normalize(values):
    floats = values.astype(jnp.float32)
    inverse = lax.rsqrt(jnp.sum(floats * floats, axis=-1, keepdims=True) + 1e-06)
    return (floats * inverse, inverse)


def tile_weights(images, texts, scale, bias, diagonal):
    logits = (
        scale
        * lax.dot_general(
            images, texts, (((1,), (1,)), ((), ())), preferred_element_type=jnp.float32
        )
        + bias
    )
    if diagonal:
        eye = jnp.arange(images.shape[0])[:, None] == jnp.arange(texts.shape[0])[None, :]
        signs = jnp.where(eye, jnp.float32(1.0), jnp.float32(-1.0))
    else:
        signs = jnp.full(logits.shape, -1.0, jnp.float32)
    coeffs = -signs * jax.nn.sigmoid(-signs * logits)
    return (scale * coeffs).astype(jnp.bfloat16)


def transposed(coeffs, images):
    return lax.dot_general(
        coeffs, images, (((0,), (0,)), ((), ())), preferred_element_type=jnp.float32
    )


def finish(unit, inverse, grads):
    return inverse * (grads - unit * jnp.sum(unit * grads, axis=-1, keepdims=True))


def per_device(img_emb, txt_emb, logit_scale, logit_bias):
    top_bit = lax.axis_size("dx").bit_length() - 2
    half = txt_emb.shape[0] // 2

    def odd(index):
        return index >> (top_bit - 1) & 1

    first, txt_emb, img_emb = lax.optimization_barrier((txt_emb[:half], txt_emb, img_emb))
    far_raw = [from_partner(first, "dx", top_bit), from_partner(txt_emb[half:], "dx", top_bit)]
    img_b, txt_b = rounded_units(img_emb, txt_emb)
    scale = logit_scale[0]
    bias = logit_bias[0]

    own_coeffs = tile_weights(img_b, txt_b, scale, bias, True)
    grad_i = jnp.dot(own_coeffs, txt_b, preferred_element_type=jnp.float32)
    grad_t = transposed(own_coeffs, img_b)

    def forward_part(far_txt):
        coeffs = tile_weights(img_b, far_txt, scale, bias, False)
        more = jnp.dot(coeffs, far_txt, preferred_element_type=jnp.float32)
        return (more, transposed(coeffs, img_b))

    near = (("dx", 0), ("dy", 0), ("dx", 1))
    near_b, own_coeffs = lax.optimization_barrier((txt_b, own_coeffs))
    near_txt = [from_partner(near_b, axis, bit) for axis, bit in near]

    def far_part(raw):
        far_unit, far_inv = normalize(raw)
        more, partial_value = forward_part(far_unit.astype(jnp.bfloat16))
        return (more, finish(far_unit, far_inv, partial_value).astype(jnp.bfloat16))

    more, partial_value = far_part(far_raw[0])
    grad_i = grad_i + more
    far_back = [from_partner(partial_value, "dx", top_bit)]
    partial_value, near_txt, img_emb, txt_emb = lax.optimization_barrier(
        (partial_value, near_txt, img_emb, txt_emb)
    )
    img_unit, inv_img = normalize(img_emb)
    txt_unit, inv_txt = normalize(txt_emb)

    near_partials = []
    for at, (axis, bit) in enumerate(near):
        more, partial_value = forward_part(near_txt[at])
        grad_i = grad_i + more
        near_partials.append(partial_value.astype(jnp.bfloat16))

    near_back = [from_partner(near_partials[0], *near[0])]
    raw, _, near_back = lax.optimization_barrier((far_raw[1], near_partials, near_back))
    more, partial_value = far_part(raw)
    grad_i = grad_i + more
    most = half * 3 // 8 // STEP * STEP
    last = half - STEP
    far_back.append(from_partner(partial_value[:most], "dx", top_bit))
    far_back.append(from_partner(partial_value[most:last], "dx", top_bit))
    rest = partial_value[last:]
    even_back = from_partner(rest, "dx", top_bit, lambda index: not odd(index))
    for (axis, bit), partial_value in zip(near[1:], near_partials[1:]):
        near_back.append(from_partner(partial_value, axis, bit))
    for partial_value in near_back:
        grad_t = grad_t + partial_value.astype(jnp.float32)
    grad_img, base, returned = lax.optimization_barrier(
        (finish(img_unit, inv_img, grad_i), finish(txt_unit, inv_txt, grad_t), far_back[0])
    )
    grad_txt = add_rows(base, [returned], (0,))
    rest, far_back[1], grad_txt, grad_img = lax.optimization_barrier(
        (rest, far_back[1], grad_txt, grad_img)
    )
    odd_back = from_partner(rest, "dx", top_bit, odd)
    grad_txt = add_rows(base, [far_back[1]], (half,), grad_txt)
    grad_txt = add_rows(base, [far_back[2]], (half + most,), grad_txt)
    grad_txt = add_rows(base, [even_back, odd_back], (half + last,), grad_txt, odd)
    return (grad_img, grad_txt)


def solution(mesh):
    return jax.shard_map(
        per_device,
        mesh=mesh,
        in_specs=(P(("dx", "dy"), None), P(("dx", "dy"), None), P(), P()),
        out_specs=(P(("dx", "dy"), None), P(("dx", "dy"), None)),
        check_vma=False,
    )
```

```python
import functools

import jax
import jax.numpy as jnp
from jax import lax
from jax.experimental import pallas as pl
from jax.experimental.pallas import tpu as pltpu
from jax.sharding import PartitionSpec as P

STEP = 32


def unit_kernel(*refs):
    for values, rounded in zip(refs[:2], refs[2:]):
        floats = values[...].astype(jnp.float32)
        inverse = lax.rsqrt(jnp.sum(floats * floats, axis=-1, keepdims=True) + 1e-06)
        rounded[...] = (floats * inverse).astype(jnp.bfloat16)


def rounded_units(*arrays):
    rows, width = arrays[0].shape
    block = pl.BlockSpec((rows // 4, width), lambda i: (i, 0))
    shape = jax.ShapeDtypeStruct((rows, width), jnp.bfloat16)
    return pl.pallas_call(
        unit_kernel,
        grid=(4,),
        out_shape=(shape, shape),
        in_specs=[block, block],
        out_specs=(block, block),
    )(*arrays)


def add_kernel(offsets, odd, base, *refs):
    parts, (out, total, sems) = refs[: len(offsets) + (odd is not None)], refs[-3:]
    copies = []
    for index, offset in enumerate(offsets):
        for at in range(parts[index].shape[0] // STEP):
            here = pl.ds(at * STEP, STEP)
            there = pl.ds(offset + at * STEP, STEP)
            slot = pl.ds(len(copies) * STEP, STEP)
            part = parts[index][here].astype(jnp.float32)
            if odd is not None and index == len(offsets) - 1:
                is_odd = odd(lax.axis_index("dx")) == 1
                part = jnp.where(is_odd, parts[index + 1][here].astype(jnp.float32), part)
            total[slot] = base[there] + part
            copies.append(
                pltpu.make_async_copy(total.at[slot], out.at[there], sems.at[len(copies)])
            )
            copies[-1].start()
    for copy in copies:
        copy.wait()


def add_rows(base, parts, offsets, out=None, odd=None):
    vmem, hbm = (pl.BlockSpec(memory_space=space) for space in (pltpu.VMEM, pltpu.HBM))
    args = [base, *parts] + ([] if out is None else [out])
    rows = sum(part.shape[0] for part in parts[: len(offsets)])
    return pl.pallas_call(
        functools.partial(add_kernel, offsets, odd),
        out_shape=jax.ShapeDtypeStruct(base.shape, jnp.float32),
        in_specs=[vmem] * (1 + len(parts)) + ([] if out is None else [hbm]),
        out_specs=hbm,
        scratch_shapes=[
            pltpu.VMEM((rows, base.shape[1]), jnp.float32),
            pltpu.SemaphoreType.DMA((rows // STEP,)),
        ],
        input_output_aliases={} if out is None else {len(args) - 1: 0},
        compiler_params=pltpu.CompilerParams(vmem_limit_bytes=16 * 2**20),
        cost_estimate=pl.CostEstimate(
            flops=rows * base.shape[1], bytes_accessed=10 * rows * base.shape[1], transcendentals=0
        ),
    )(*args)


def from_partner(value, axis, stride, among=lambda index: True):
    pairs = [(i, i ^ 1 << stride) for i in range(lax.axis_size(axis)) if among(i)]
    return lax.ppermute(value, axis, pairs)


def normalize(values):
    floats = values.astype(jnp.float32)
    inverse = lax.rsqrt(jnp.sum(floats * floats, axis=-1, keepdims=True) + 1e-06)
    return (floats * inverse, inverse)


def tile_weights(images, texts, scale, bias, diagonal):
    logits = (
        scale
        * lax.dot_general(
            images, texts, (((1,), (1,)), ((), ())), preferred_element_type=jnp.float32
        )
        + bias
    )
    if diagonal:
        eye = jnp.arange(images.shape[0])[:, None] == jnp.arange(texts.shape[0])[None, :]
        signs = jnp.where(eye, jnp.float32(1.0), jnp.float32(-1.0))
    else:
        signs = jnp.full(logits.shape, -1.0, jnp.float32)
    coeffs = -signs * jax.nn.sigmoid(-signs * logits)
    return (scale * coeffs).astype(jnp.bfloat16)


def transposed(coeffs, images):
    return lax.dot_general(
        coeffs, images, (((0,), (0,)), ((), ())), preferred_element_type=jnp.float32
    )


def finish(unit, inverse, grads):
    return inverse * (grads - unit * jnp.sum(unit * grads, axis=-1, keepdims=True))


def per_device(img_emb, txt_emb, logit_scale, logit_bias):
    top_bit = lax.axis_size("dx").bit_length() - 2
    half = txt_emb.shape[0] * 7 // 16 // STEP * STEP
    second = txt_emb.shape[0] - half

    def odd(index):
        return index >> (top_bit - 1) & 1

    first, txt_emb, img_emb = lax.optimization_barrier((txt_emb[:half], txt_emb, img_emb))
    far_raw = [from_partner(first, "dx", top_bit), from_partner(txt_emb[half:], "dx", top_bit)]
    img_b, txt_b = rounded_units(img_emb, txt_emb)
    scale = logit_scale[0]
    bias = logit_bias[0]

    own_coeffs = tile_weights(img_b, txt_b, scale, bias, True)
    grad_i = jnp.dot(own_coeffs, txt_b, preferred_element_type=jnp.float32)
    grad_t = transposed(own_coeffs, img_b)

    def forward_part(far_txt):
        coeffs = tile_weights(img_b, far_txt, scale, bias, False)
        more = jnp.dot(coeffs, far_txt, preferred_element_type=jnp.float32)
        return (more, transposed(coeffs, img_b))

    near = (("dx", 0), ("dy", 0), ("dx", 1))
    near_b, own_coeffs = lax.optimization_barrier((txt_b, own_coeffs))
    near_txt = [from_partner(near_b, axis, bit) for axis, bit in near]

    def far_part(raw):
        far_unit, far_inv = normalize(raw)
        more, partial_value = forward_part(far_unit.astype(jnp.bfloat16))
        return (more, finish(far_unit, far_inv, partial_value).astype(jnp.bfloat16))

    more, partial_value = far_part(far_raw[0])
    grad_i = grad_i + more
    far_back = [from_partner(partial_value, "dx", top_bit)]
    partial_value, near_txt, img_emb, txt_emb = lax.optimization_barrier(
        (partial_value, near_txt, img_emb, txt_emb)
    )
    img_unit, inv_img = normalize(img_emb)
    txt_unit, inv_txt = normalize(txt_emb)

    near_partials = []
    for at, (axis, bit) in enumerate(near):
        more, partial_value = forward_part(near_txt[at])
        grad_i = grad_i + more
        near_partials.append(partial_value.astype(jnp.bfloat16))

    near_back = [from_partner(near_partials[0], *near[0])]
    raw, _, near_back = lax.optimization_barrier((far_raw[1], near_partials, near_back))
    more, partial_value = far_part(raw)
    grad_i = grad_i + more
    most = second - 5 * STEP
    last = second - STEP
    far_back.append(from_partner(partial_value[:most], "dx", top_bit))
    far_back.append(from_partner(partial_value[most:last], "dx", top_bit))
    rest = partial_value[last:]
    even_back = from_partner(rest, "dx", top_bit, lambda index: not odd(index))
    for (axis, bit), partial_value in zip(near[1:], near_partials[1:]):
        near_back.append(from_partner(partial_value, axis, bit))
    for partial_value in near_back:
        grad_t = grad_t + partial_value.astype(jnp.float32)
    grad_img, base, returned = lax.optimization_barrier(
        (finish(img_unit, inv_img, grad_i), finish(txt_unit, inv_txt, grad_t), far_back[0])
    )
    grad_txt = add_rows(base, [returned], (0,))
    rest, far_back[1], grad_txt, grad_img = lax.optimization_barrier(
        (rest, far_back[1], grad_txt, grad_img)
    )
    odd_back = from_partner(rest, "dx", top_bit, odd)
    grad_txt = add_rows(base, [far_back[1]], (half,), grad_txt)
    grad_txt = add_rows(base, [far_back[2]], (half + most,), grad_txt)
    grad_txt = add_rows(base, [even_back, odd_back], (half + last,), grad_txt, odd)
    return (grad_img, grad_txt)


def solution(mesh):
    return jax.shard_map(
        per_device,
        mesh=mesh,
        in_specs=(P(("dx", "dy"), None), P(("dx", "dy"), None), P(), P()),
        out_specs=(P(("dx", "dy"), None), P(("dx", "dy"), None)),
        check_vma=False,
    )
```

```python
import functools

import jax
import jax.numpy as jnp
from jax import lax
from jax.experimental import pallas as pl
from jax.experimental.pallas import tpu as pltpu
from jax.sharding import PartitionSpec as P

STEP = 32


def unit_kernel(*refs):
    for values, rounded in zip(refs[:2], refs[2:]):
        floats = values[...].astype(jnp.float32)
        inverse = lax.rsqrt(jnp.sum(floats * floats, axis=-1, keepdims=True) + 1e-06)
        rounded[...] = (floats * inverse).astype(jnp.bfloat16)


def rounded_units(*arrays):
    rows, width = arrays[0].shape
    block = pl.BlockSpec((rows // 4, width), lambda i: (i, 0))
    shape = jax.ShapeDtypeStruct((rows, width), jnp.bfloat16)
    return pl.pallas_call(
        unit_kernel,
        grid=(4,),
        out_shape=(shape, shape),
        in_specs=[block, block],
        out_specs=(block, block),
    )(*arrays)


def add_kernel(offsets, odd, base, *refs):
    parts, (out, total, sems) = refs[: len(offsets) + (odd is not None)], refs[-3:]
    copies = []
    for index, offset in enumerate(offsets):
        for at in range(parts[index].shape[0] // STEP):
            here = pl.ds(at * STEP, STEP)
            there = pl.ds(offset + at * STEP, STEP)
            slot = pl.ds(len(copies) * STEP, STEP)
            part = parts[index][here].astype(jnp.float32)
            if odd is not None and index == len(offsets) - 1:
                is_odd = odd(lax.axis_index("dx")) == 1
                part = jnp.where(is_odd, parts[index + 1][here].astype(jnp.float32), part)
            total[slot] = base[there] + part
            copies.append(
                pltpu.make_async_copy(total.at[slot], out.at[there], sems.at[len(copies)])
            )
            copies[-1].start()
    for copy in copies:
        copy.wait()


def add_rows(base, parts, offsets, out=None, odd=None):
    vmem, hbm = (pl.BlockSpec(memory_space=space) for space in (pltpu.VMEM, pltpu.HBM))
    args = [base, *parts] + ([] if out is None else [out])
    rows = sum(part.shape[0] for part in parts[: len(offsets)])
    return pl.pallas_call(
        functools.partial(add_kernel, offsets, odd),
        out_shape=jax.ShapeDtypeStruct(base.shape, jnp.float32),
        in_specs=[vmem] * (1 + len(parts)) + ([] if out is None else [hbm]),
        out_specs=hbm,
        scratch_shapes=[
            pltpu.VMEM((rows, base.shape[1]), jnp.float32),
            pltpu.SemaphoreType.DMA((rows // STEP,)),
        ],
        input_output_aliases={} if out is None else {len(args) - 1: 0},
        compiler_params=pltpu.CompilerParams(vmem_limit_bytes=16 * 2**20),
        cost_estimate=pl.CostEstimate(
            flops=rows * base.shape[1], bytes_accessed=10 * rows * base.shape[1], transcendentals=0
        ),
    )(*args)


def from_partner(value, axis, stride, among=lambda index: True):
    pairs = [(i, i ^ 1 << stride) for i in range(lax.axis_size(axis)) if among(i)]
    return lax.ppermute(value, axis, pairs)


def normalize(values):
    floats = values.astype(jnp.float32)
    inverse = lax.rsqrt(jnp.sum(floats * floats, axis=-1, keepdims=True) + 1e-06)
    return (floats * inverse, inverse)


def tile_weights(images, texts, scale, bias, diagonal):
    logits = (
        scale
        * lax.dot_general(
            images, texts, (((1,), (1,)), ((), ())), preferred_element_type=jnp.float32
        )
        + bias
    )
    if diagonal:
        eye = jnp.arange(images.shape[0])[:, None] == jnp.arange(texts.shape[0])[None, :]
        signs = jnp.where(eye, jnp.float32(1.0), jnp.float32(-1.0))
    else:
        signs = jnp.full(logits.shape, -1.0, jnp.float32)
    coeffs = -signs * jax.nn.sigmoid(-signs * logits)
    return (scale * coeffs).astype(jnp.bfloat16)


def transposed(coeffs, images):
    return lax.dot_general(
        coeffs, images, (((0,), (0,)), ((), ())), preferred_element_type=jnp.float32
    )


def finish(unit, inverse, grads):
    return inverse * (grads - unit * jnp.sum(unit * grads, axis=-1, keepdims=True))


def per_device(img_emb, txt_emb, logit_scale, logit_bias):
    top_bit = lax.axis_size("dx").bit_length() - 2
    half = txt_emb.shape[0] * 7 // 16 // STEP * STEP
    second = txt_emb.shape[0] - half

    def odd(index):
        return index >> (top_bit - 1) & 1

    first, txt_emb, img_emb = lax.optimization_barrier((txt_emb[:half], txt_emb, img_emb))
    far_raw = [from_partner(first, "dx", top_bit), from_partner(txt_emb[half:], "dx", top_bit)]
    img_b, txt_b = rounded_units(img_emb, txt_emb)
    scale = logit_scale[0]
    bias = logit_bias[0]

    own_coeffs = tile_weights(img_b, txt_b, scale, bias, True)
    grad_i = jnp.dot(own_coeffs, txt_b, preferred_element_type=jnp.float32)
    grad_t = transposed(own_coeffs, img_b)

    def forward_part(far_txt):
        coeffs = tile_weights(img_b, far_txt, scale, bias, False)
        more = jnp.dot(coeffs, far_txt, preferred_element_type=jnp.float32)
        return (more, transposed(coeffs, img_b))

    near = (("dx", 0), ("dy", 0), ("dx", 1))
    near_b, own_coeffs = lax.optimization_barrier((txt_b, own_coeffs))
    near_txt = [from_partner(near_b, axis, bit) for axis, bit in near]

    def far_part(raw):
        far_unit, far_inv = normalize(raw)
        more, partial_value = forward_part(far_unit.astype(jnp.bfloat16))
        return (more, finish(far_unit, far_inv, partial_value).astype(jnp.bfloat16))

    more, partial_value = far_part(far_raw[0])
    grad_i = grad_i + more
    far_back = [from_partner(partial_value, "dx", top_bit)]
    partial_value, near_txt, img_emb, txt_emb = lax.optimization_barrier(
        (partial_value, near_txt, img_emb, txt_emb)
    )
    img_unit, inv_img = normalize(img_emb)
    txt_unit, inv_txt = normalize(txt_emb)

    near_partials = []
    for at, (axis, bit) in enumerate(near):
        more, partial_value = forward_part(near_txt[at])
        grad_i = grad_i + more
        near_partials.append(partial_value.astype(jnp.bfloat16))

    near_back = [from_partner(near_partials[0], *near[0])]
    raw, _, near_back = lax.optimization_barrier((far_raw[1], near_partials, near_back))
    more, partial_value = far_part(raw)
    grad_i = grad_i + more
    most = second - 5 * STEP
    last = second - STEP
    far_back.append(from_partner(partial_value[:most], "dx", top_bit))
    far_back.append(from_partner(partial_value[most:last], "dx", top_bit))
    rest = partial_value[last:]
    even_back = from_partner(rest, "dx", top_bit, lambda index: not odd(index))
    for (axis, bit), partial_value in zip(near[1:], near_partials[1:]):
        near_back.append(from_partner(partial_value, axis, bit))
    for partial_value in near_back:
        grad_t = grad_t + partial_value.astype(jnp.float32)
    grad_img, base, returned = lax.optimization_barrier(
        (finish(img_unit, inv_img, grad_i), finish(txt_unit, inv_txt, grad_t), far_back[0])
    )
    grad_txt = add_rows(base, [returned], (0,))
    rest, far_back[1], grad_txt, grad_img = lax.optimization_barrier(
        (rest, far_back[1], grad_txt, grad_img)
    )
    odd_back = from_partner(rest, "dx", top_bit, odd)
    grad_txt = add_rows(base, [far_back[1]], (half,), grad_txt)
    grad_txt = add_rows(base, [far_back[2]], (half + most,), grad_txt)
    end = base[half + last :] + (even_back.astype(jnp.float32) + odd_back.astype(jnp.float32))
    grad_txt = lax.dynamic_update_slice(grad_txt, end, (half + last, 0))
    return (grad_img, grad_txt)


def solution(mesh):
    return jax.shard_map(
        per_device,
        mesh=mesh,
        in_specs=(P(("dx", "dy"), None), P(("dx", "dy"), None), P(), P()),
        out_specs=(P(("dx", "dy"), None), P(("dx", "dy"), None)),
        check_vma=False,
    )
```
